1024 devices in a mesh: blk: 32 (over z, x_hi), inner: 32 (over y, x_lo, core).
Axes of the slice: x: 8 (x_hi: 4, x_lo: 2; x = x_hi * 2 + x_lo), y: 8, z: 8, core: 2. Of those that a mesh axis runs over, the one named last changes fastest.
Arguments:
- image_student: bfloat16 [229376, 1152], P(('blk', 'inner')), may hold values from -6 to 6
- text_student: bfloat16 [229376, 1152], P(('blk', 'inner')), may hold values from -6 to 6
- image_teacher: bfloat16 [229376, 1152], P(('blk', 'inner')), may hold values from -6 to 6
- text_teacher: bfloat16 [229376, 1152], P(('blk', 'inner')), may hold values from -6 to 6
- pair_ids: int32 [229376], replicated, may hold values from 0 to 28671
Outputs:
- image_grad: bfloat16 [229376, 1152], P(('blk', 'inner'))
- text_grad: bfloat16 [229376, 1152], P(('blk', 'inner'))
The draws below stay inside these ranges and needn't reach their ends.
Inputs may be any that keep to these rules, and one draw needn't show every extreme that they name: Image row i and text row j form a positive pair exactly when pair_ids[i] == pair_ids[j]; every row is positive with its own text.
All inputs are finite; a program needn't handle non-finite values.
Results may differ from the reference program's by a relative error of at most 0.012.
Values may be sent and summed in bfloat16 or wider, within the bound.
A program may use at most 32 MiB of HBM per device.

```python
import jax
import jax.numpy as jnp
from jax import lax

D = 1152
TOK_DEV = 224
WINDOW = 4
TOKENS = 229376
N_BLK = 32
N_INNER = 32


def set_ends(entries, key, low, high):
    index_at = [jax.random.randint(jax.random.fold_in(key, axis), (), 0, length) for axis, length in enumerate(entries.shape)]
    main_axis = entries.shape.index(max(entries.shape))
    beside = index_at[:main_axis] + [(index_at[main_axis] + 1) % entries.shape[main_axis]] + index_at[main_axis + 1:]
    return entries.at[tuple(index_at)].set(low).at[tuple(beside)].set(high)


def level_of(key, extent, shards, low, top_value):
    level = 1.0
    for position, parts in shards:
        heights = jax.random.uniform(jax.random.fold_in(jax.random.fold_in(key, 6), position), (parts,), jnp.float32, low / len(shards), top_value / len(shards))
        level = level * jnp.repeat(jnp.exp(heights), extent[position] // parts).reshape((-1,) + (1,) * (len(extent) - 1 - position))
    return level


def bell_draw(key, extent, scale, reach, split=(), held_as=jnp.bfloat16):
    result = scale * jax.random.normal(key, extent, jnp.float32)
    if split:
        result = result * level_of(key, extent, split, -0.22, 0.18)
    return jnp.clip(result, -reach, reach).astype(held_as)


def setup_inputs(seed: int = 0) -> dict:
    key_of = jax.random.split(jax.random.key(seed), 6)
    return {
        "image_student": bell_draw(key_of[0], (TOKENS, D), 1.0, 6.0, ((0, 1024),)),
        "text_student": bell_draw(key_of[1], (TOKENS, D), 1.0, 6.0, ((0, 1024),)),
        "image_teacher": bell_draw(key_of[2], (TOKENS, D), 1.0, 6.0, ((0, 1024),)),
        "text_teacher": bell_draw(key_of[3], (TOKENS, D), 1.0, 6.0, ((0, 1024),)),
        "pair_ids": set_ends(jax.random.randint(key_of[4], (TOKENS,), 0, TOKENS // 8), jax.random.fold_in(key_of[4], 1), 0, (TOKENS // 8) - 1).astype(jnp.int32),
    }


logit_gain = 32.0
logit_shift = -2.0


def signal_block(img_s, img_t, ids_img, txt_s, txt_t, ids_txt):
    width = img_s.shape[1]
    student = (logit_gain / width) * jnp.dot(img_s, txt_s.T, preferred_element_type=jnp.float32) + logit_shift
    teacher = (logit_gain / width) * jnp.dot(img_t, txt_t.T, preferred_element_type=jnp.float32) + logit_shift
    same = (ids_img[:, None] == ids_txt[None, :]).astype(jnp.float32)
    target = 0.5 * same + 0.5 * jax.nn.sigmoid(teacher)
    return (jax.nn.sigmoid(student) - target).astype(jnp.bfloat16)


def reference(image_student, text_student, image_teacher, text_teacher, pair_ids):
    count = N_BLK * N_INNER
    width = image_student.shape[1]

    def block(arr, index):
        return lax.dynamic_slice_in_dim(arr, (index * TOK_DEV).astype(jnp.int32), TOK_DEV, 0)

    def image_side(k):
        total = jnp.zeros((TOK_DEV, width), jnp.float32)
        for s in range(WINDOW):
            j = ((k - s) % count).astype(jnp.int32)
            signal = signal_block(block(image_student, k), block(image_teacher, k), block(pair_ids, k),
                                  block(text_student, j), block(text_teacher, j), block(pair_ids, j))
            total = total + jnp.dot(signal, block(text_student, j), preferred_element_type=jnp.float32)
        return ((logit_gain / width) * total).astype(jnp.bfloat16)

    def text_side(j):
        total = jnp.zeros((TOK_DEV, width), jnp.float32)
        for s in range(WINDOW):
            k = ((j + s) % count).astype(jnp.int32)
            signal = signal_block(block(image_student, k), block(image_teacher, k), block(pair_ids, k),
                                  block(text_student, j), block(text_teacher, j), block(pair_ids, j))
            total = total + jnp.dot(signal.T, block(image_student, k), preferred_element_type=jnp.float32)
        return ((logit_gain / width) * total).astype(jnp.bfloat16)

    blocks = jnp.arange(count, dtype=jnp.int32)
    image_grad = lax.map(image_side, blocks).reshape(TOKENS, width)
    text_grad = lax.map(text_side, blocks).reshape(TOKENS, width)
    return image_grad, text_grad
```

```python
import functools

import jax
import jax.numpy as jnp
from jax import lax
from jax.experimental import pallas as pl
from jax.experimental.pallas import tpu as pltpu
from jax.sharding import PartitionSpec as P

MESH = pl.DeviceIdType.MESH
LANES = 128
PARTS = 2

logit_gain = 32.0
logit_shift = -2.0


def kernel(
    n_blk, n_inner, img_s, txt_s, img_t, txt_t, ids, image_grad, text_grad,
    IS, IT, TS, TT, XS, XT, SIG, SIGX, IDS, COL, H_OWN, H_ACC, H_SUM, H1S, H2S, H1R, H2R,
    G_OWN, GS, GR, GXS, GXR, G_OUT, H_OUT,
    load_sem, img_sem, x_sem, p1_send, p1_recv, p2_send, p2_recv, fwd_send,
    h1_sem, h2_sem, g_sem, gx_sem, out_sem,
):
    rows, width = img_s.shape
    part = rows // PARTS
    gain = logit_gain / width
    n_dev = n_blk * n_inner
    blk, inner = lax.axis_index("blk"), lax.axis_index("inner")
    g = blk * n_inner + inner
    core = lax.rem(inner, 2)
    right_x = lax.rem(inner // 2, 2) == 1
    y = inner // 4
    top, bottom = y == n_inner // 4 - 1, y == 0
    c0, c1 = core == 0, core == 1
    no = jnp.logical_not

    has_p2 = c1 & no(bottom)
    forwards = has_p2 & right_x
    sends_p2 = c1 & no(top)
    sends_p1 = no(sends_p2 & right_x)
    gets_x = c1 & ((right_x & top) | (no(right_x) & bottom))
    sends_x = c0 & bottom

    def block(shift):
        return lax.rem(g + shift + n_dev, n_dev)

    def at(shift):
        b = block(shift)
        return (b // n_inner, lax.rem(b, n_inner))

    mate = (blk, inner + 1 - 2 * core)
    after, before, after2, before2 = at(2), at(-2), at(4), at(-4)
    step_up, step_down = at(1), at(-1)

    def piece(r):
        return pl.ds(r * part, part)

    def remote(src, dst, send, recv, to):
        return pltpu.make_async_remote_copy(
            src_ref=src, dst_ref=dst, send_sem=send, recv_sem=recv, device_id=to, device_id_type=MESH
        )

    loads = [
        pltpu.make_async_copy(src, dst, load_sem.at[i])
        for i, (src, dst) in enumerate(
            ((txt_s, TS.at[0]), (img_s, IS.at[0]), (txt_t, TT.at[0]), (img_t, IT.at[0]), (ids, IDS))
        )
    ]
    to_mate = [
        remote(src, dst, img_sem.at[0, i], img_sem.at[1, i], mate)
        for i, (src, dst) in enumerate(((img_s, IS.at[1]), (img_t, IT.at[1])))
    ]
    to_x = [
        remote(src, dst, x_sem.at[0, i], x_sem.at[1, i], step_down)
        for i, (src, dst) in enumerate(((img_s, XS), (img_t, XT)))
    ]
    p1, p2, fwd = {}, {}, {}
    for r in range(PARTS):
        for i, (src, held) in enumerate(((txt_s, TS), (txt_t, TT))):
            k = 2 * r + i
            p1[r, i] = remote(src.at[piece(r)], held.at[1, piece(r)], p1_send.at[k], p1_recv.at[k], after)
            p2[r, i] = remote(src.at[piece(r)], held.at[2, piece(r)], p2_send.at[k], p2_recv.at[k], after2)
            fwd[r, i] = remote(
                held.at[2, piece(r)], held.at[1, piece(r)], fwd_send.at[k], p1_recv.at[k], before
            )
    h1 = [remote(H1S.at[piece(r)], H1R.at[piece(r)], h1_sem.at[0, r], h1_sem.at[1, r], before) for r in range(PARTS)]
    h2 = [remote(H2S.at[piece(r)], H2R.at[piece(r)], h2_sem.at[0, r], h2_sem.at[1, r], before2) for r in range(PARTS)]
    g_copy = remote(GS, GR, g_sem.at[0], g_sem.at[1], mate)
    gx_copy = remote(GXS, GXR, gx_sem.at[0], gx_sem.at[1], step_up)
    g_out = pltpu.make_async_copy(G_OUT, image_grad, out_sem.at[PARTS])
    h_out = [
        pltpu.make_async_copy(H_OUT.at[piece(r)], text_grad.at[piece(r)], out_sem.at[r]) for r in range(PARTS)
    ]

    barrier = pltpu.get_barrier_semaphore()

    def greet(to):
        pl.semaphore_signal(barrier, inc=1, device_id=to, device_id_type=MESH)

    for to in (after, before, mate):
        greet(to)

    @pl.when(c1)
    def _():
        greet(after2)
        greet(before2)

    @pl.when(gets_x)
    def _():
        greet(step_up)

    @pl.when(sends_x)
    def _():
        greet(step_down)

    for copy in loads:
        copy.start()
    peers = 3 + 2 * core + jnp.where(gets_x | sends_x, 1, 0)
    pl.semaphore_wait(barrier, peers)

    @pl.when(sends_p1)
    def _():
        for key in p1:
            p1[key].start()

    @pl.when(sends_p2)
    def _():
        for key in p2:
            p2[key].start()

    for copy in to_mate:
        copy.start()

    @pl.when(sends_x)
    def _():
        for copy in to_x:
            copy.start()

    for copy in loads:
        copy.wait()

    def lane_ids(b):
        start = b * rows
        first = jnp.minimum(start // LANES, IDS.shape[0] - 3)
        offset = start - first * LANES
        line = jnp.concatenate([IDS[pl.ds(first + i, 1), :] for i in range(3)], axis=1)
        line = jnp.broadcast_to(line.astype(jnp.float32), (8, 3 * LANES))
        return pltpu.roll(line, lax.rem(3 * LANES - offset, 3 * LANES), 1)[0:1]

    even = g - core
    own_ids = lane_ids(g)[:, :rows]
    mate_ids = lane_ids(even + 1 - core)[:, :rows]
    x_ids = lane_ids(block(1))[:, :rows]
    for q, b in enumerate((g, block(-2), block(-4))):
        COL[q] = jnp.transpose(jnp.broadcast_to(lane_ids(b)[:, : 2 * LANES], (LANES, 2 * LANES)))

    def nt(a, b):
        return lax.dot_general(a, b, (((1,), (1,)), ((), ())), preferred_element_type=jnp.float32)

    def tn(a, b):
        return lax.dot_general(a, b, (((0,), (0,)), ((), ())), preferred_element_type=jnp.float32)

    def nn(a, b):
        return jnp.dot(a, b, preferred_element_type=jnp.float32)

    def signal(q, r, student_img, teacher_img, img_ids):
        span = pl.ds(0, rows) if r is None else piece(r)
        student = (0.5 * gain) * nt(TS[q, span], student_img[...]) + 0.5 * logit_shift
        teacher = (0.5 * gain) * nt(TT[q, span], teacher_img[...]) + 0.5 * logit_shift
        same = jnp.where(COL[q, span, 0:1] == img_ids, 0.5, 0.0)
        target = same + (0.25 + 0.25 * jnp.tanh(teacher))
        return ((0.5 + 0.5 * jnp.tanh(student)) - target).astype(jnp.bfloat16)

    own = signal(0, None, IS.at[0], IT.at[0], own_ids)
    SIG[0, 0] = own
    H_OWN[...] = nn(own, IS[0])
    for copy in to_mate:
        copy.wait_recv()

    @pl.when(c0)
    def _():
        other = signal(0, None, IS.at[1], IT.at[1], mate_ids)
        SIG[0, 1] = other
        H_OWN[...] += nn(other, IS[1])

    def second(r):
        for i in range(2):
            p2[r, i].wait_recv()

            @pl.when(forwards)
            def _():
                fwd[r, i].start()

        other = signal(2, r, IS.at[1], IT.at[1], mate_ids)
        SIG[2, 1, piece(r)] = other
        H2S[piece(r)] = nn(other, IS[1]).astype(jnp.bfloat16)
        h2[r].start()

    def first(r):
        for i in range(2):
            p1[r, i].wait_recv()
        near = signal(1, r, IS.at[0], IT.at[0], own_ids)
        SIG[1, 0, piece(r)] = near
        other = signal(1, r, IS.at[1], IT.at[1], mate_ids)
        SIG[1, 1, piece(r)] = other
        H_ACC[...] = nn(near, IS[0]) + nn(other, IS[1])

        @pl.when(gets_x)
        def _():
            if r == 0:
                for copy in to_x:
                    copy.wait_recv()
            far = signal(1, r, XS, XT, x_ids)
            SIGX[piece(r)] = far
            H_ACC[...] += nn(far, XS[...])

        H1S[piece(r)] = H_ACC[...].astype(jnp.bfloat16)
        h1[r].start()

    @pl.when(has_p2)
    def _():
        second(0)

    @pl.when(has_p2 & right_x)
    def _():
        second(1)

    first(0)

    @pl.when(has_p2 & no(right_x))
    def _():
        second(1)

    first(1)

    @pl.when(gets_x)
    def _():
        GXS[...] = tn(SIGX[...], TS[1]).astype(jnp.bfloat16)
        gx_copy.start()

    G_OWN[...] = tn(SIG[1, 1], TS[1])

    @pl.when(c0)
    def _():
        G_OWN[...] += tn(SIG[0, 1], TS[0])

    @pl.when(has_p2)
    def _():
        G_OWN[...] += tn(SIG[2, 1], TS[2])

    GS[...] = G_OWN[...].astype(jnp.bfloat16)
    g_copy.start()
    G_OWN[...] = tn(SIG[0, 0], TS[0]) + tn(SIG[1, 0], TS[1])

    @pl.when(sends_x)
    def _():
        gx_copy.wait_recv()
        G_OWN[...] += GXR[...].astype(jnp.float32)

    g_copy.wait_recv()
    G_OUT[...] = (gain * (G_OWN[...] + GR[...].astype(jnp.float32))).astype(jnp.bfloat16)
    g_out.start()

    for r in range(PARTS):
        @pl.when(sends_p2)
        def _():
            h2[r].wait_recv()
            H_OWN[piece(r)] += H2R[piece(r)].astype(jnp.float32)

        h1[r].wait_recv()
        H_OUT[piece(r)] = (gain * (H_OWN[piece(r)] + H1R[piece(r)].astype(jnp.float32))).astype(jnp.bfloat16)
        h_out[r].start()

    for copy in to_mate + h1 + [g_copy]:
        copy.wait_send()

    @pl.when(sends_p1)
    def _():
        for key in p1:
            p1[key].wait_send()

    @pl.when(sends_p2)
    def _():
        for key in p2:
            p2[key].wait_send()

    @pl.when(forwards)
    def _():
        for key in fwd:
            fwd[key].wait_send()

    @pl.when(has_p2)
    def _():
        for copy in h2:
            copy.wait_send()

    @pl.when(sends_x)
    def _():
        for copy in to_x:
            copy.wait_send()

    @pl.when(gets_x)
    def _():
        gx_copy.wait_send()

    for copy in h_out + [g_out]:
        copy.wait()


def local(n_blk, n_inner, image_student, text_student, image_teacher, text_teacher, pair_ids):
    rows, width = image_student.shape
    bf, f32 = jnp.bfloat16, jnp.float32
    VM, DMA = pltpu.VMEM, pltpu.SemaphoreType.DMA
    ids = pair_ids.reshape(-1, LANES)
    part = rows // PARTS
    one = (rows, width)
    return pl.pallas_call(
        functools.partial(kernel, n_blk, n_inner),
        out_shape=(jax.ShapeDtypeStruct(one, bf), jax.ShapeDtypeStruct(one, bf)),
        in_specs=[pl.BlockSpec(memory_space=pl.ANY)] * 5,
        out_specs=(pl.BlockSpec(memory_space=pl.ANY),) * 2,
        scratch_shapes=[
            VM((2, *one), bf), VM((2, *one), bf),
            VM((3, *one), bf), VM((3, *one), bf),
            VM(one, bf), VM(one, bf),
            VM((3, 2, rows, rows), bf), VM((rows, rows), bf),
            VM(ids.shape, jnp.int32), VM((3, 2 * LANES, LANES), f32),
            VM(one, f32), VM((part, width), f32), VM((8, LANES), f32),
            VM(one, bf), VM(one, bf), VM(one, bf), VM(one, bf),
            VM(one, f32), VM(one, bf), VM(one, bf), VM(one, bf), VM(one, bf),
            VM(one, bf), VM(one, bf),
            DMA((5,)), DMA((2, 2)), DMA((2, 2)),
            DMA((2 * PARTS,)), DMA((2 * PARTS,)), DMA((2 * PARTS,)), DMA((2 * PARTS,)), DMA((2 * PARTS,)),
            DMA((2, PARTS)), DMA((2, PARTS)), DMA((2,)), DMA((2,)), DMA((PARTS + 1,)),
        ],
        compiler_params=pltpu.CompilerParams(
            collective_id=0, has_side_effects=True, vmem_limit_bytes=48 << 20
        ),
        name="window_grads",
    )(image_student, text_student, image_teacher, text_teacher, ids)


def solution(mesh):
    both = P(("blk", "inner"), None)
    return jax.shard_map(
        functools.partial(local, mesh.shape["blk"], mesh.shape["inner"]),
        mesh=mesh,
        in_specs=(both, both, both, both, P()),
        out_specs=(both, both),
        check_vma=False,
    )
```

```python
import functools

import jax
import jax.numpy as jnp
from jax import lax
from jax.experimental import pallas as pl
from jax.experimental.pallas import tpu as pltpu
from jax.sharding import PartitionSpec as P

MESH = pl.DeviceIdType.MESH
LANES = 128
PARTS = 2

logit_gain = 32.0
logit_shift = -2.0


def kernel(
    n_blk, n_inner, img_s, txt_s, img_t, txt_t, ids, image_grad, text_grad,
    IS, IT, TS, TT, XS, XT, SIG, SIGX, IDS, COL, H_OWN, H_ACC, H1S, H2S, H1R, H2R,
    G_OWN, GS, GR, GXS, GXR, G_OUT, H_OUT,
    load_sem, img_sem, x_sem, p1_send, p1_recv, p2_send, p2_recv, fwd_send,
    h1_sem, h2_sem, g_sem, gx_sem, out_sem,
):
    rows, width = img_s.shape
    part = rows // PARTS
    gain = logit_gain / width
    n_dev = n_blk * n_inner
    blk, inner = lax.axis_index("blk"), lax.axis_index("inner")
    g = blk * n_inner + inner
    core = lax.rem(inner, 2)
    right_x = lax.rem(inner // 2, 2) == 1
    y = inner // 4
    top, bottom = y == n_inner // 4 - 1, y == 0
    c0, c1 = core == 0, core == 1
    no = jnp.logical_not

    has_p2 = c1 & no(bottom)
    forwards = has_p2 & right_x
    sends_p2 = c1 & no(top)
    sends_p1 = no(sends_p2 & right_x)
    gets_x = c1 & ((right_x & top) | (no(right_x) & bottom))
    sends_x = c0 & bottom

    def block(shift):
        return lax.rem(g + shift + n_dev, n_dev)

    def at(shift):
        b = block(shift)
        return (b // n_inner, lax.rem(b, n_inner))

    mate = (blk, inner + 1 - 2 * core)
    after, before, after2, before2 = at(2), at(-2), at(4), at(-4)
    step_up, step_down = at(1), at(-1)

    def piece(r):
        return pl.ds(r * part, part)

    def remote(src, dst, send, recv, to):
        return pltpu.make_async_remote_copy(
            src_ref=src, dst_ref=dst, send_sem=send, recv_sem=recv, device_id=to, device_id_type=MESH
        )

    loads = [
        pltpu.make_async_copy(src, dst, load_sem.at[i])
        for i, (src, dst) in enumerate(
            ((txt_s, TS.at[0]), (img_s, IS.at[0]), (txt_t, TT.at[0]), (img_t, IT.at[0]), (ids, IDS))
        )
    ]
    to_mate = [
        remote(src, dst, img_sem.at[0, i], img_sem.at[1, i], mate)
        for i, (src, dst) in enumerate(((img_s, IS.at[1]), (img_t, IT.at[1])))
    ]
    to_x = [
        remote(src, dst, x_sem.at[0, i], x_sem.at[1, i], step_down)
        for i, (src, dst) in enumerate(((img_s, XS), (img_t, XT)))
    ]
    p1, p2, fwd = {}, {}, {}
    for r in range(PARTS):
        for i, (src, held) in enumerate(((txt_s, TS), (txt_t, TT))):
            k = 2 * r + i
            p1[r, i] = remote(src.at[piece(r)], held.at[1, piece(r)], p1_send.at[k], p1_recv.at[k], after)
            p2[r, i] = remote(src.at[piece(r)], held.at[2, piece(r)], p2_send.at[k], p2_recv.at[k], after2)
            fwd[r, i] = remote(
                held.at[2, piece(r)], held.at[1, piece(r)], fwd_send.at[k], p1_recv.at[k], before
            )
    h1 = [remote(H1S.at[piece(r)], H1R.at[piece(r)], h1_sem.at[0, r], h1_sem.at[1, r], before) for r in range(PARTS)]
    h2 = [remote(H2S.at[piece(r)], H2R.at[piece(r)], h2_sem.at[0, r], h2_sem.at[1, r], before2) for r in range(PARTS)]
    g_copy = remote(GS, GR, g_sem.at[0], g_sem.at[1], mate)
    gx_copy = remote(GXS, GXR, gx_sem.at[0], gx_sem.at[1], step_up)
    g_out = pltpu.make_async_copy(G_OUT, image_grad, out_sem.at[PARTS])
    h_out = [
        pltpu.make_async_copy(H_OUT.at[piece(r)], text_grad.at[piece(r)], out_sem.at[r]) for r in range(PARTS)
    ]

    barrier = pltpu.get_barrier_semaphore()

    def greet(to):
        pl.semaphore_signal(barrier, inc=1, device_id=to, device_id_type=MESH)

    greet(mate)
    greet(before)

    @pl.when(has_p2)
    def _():
        greet(before2)

    @pl.when(has_p2 & no(right_x))
    def _():
        greet(after)

    for copy in loads:
        copy.start()
    peers = 2 + jnp.where(sends_p2, 1, 0) + jnp.where(forwards, 1, 0)
    pl.semaphore_wait(barrier, peers)

    @pl.when(sends_p1)
    def _():
        for key in p1:
            p1[key].start()

    @pl.when(sends_p2)
    def _():
        for key in p2:
            p2[key].start()

    for copy in to_mate:
        copy.start()

    for copy in loads:
        copy.wait()

    def lane_ids(b):
        start = b * rows
        first = jnp.minimum(start // LANES, IDS.shape[0] - 3)
        offset = start - first * LANES
        line = jnp.concatenate([IDS[pl.ds(first + i, 1), :] for i in range(3)], axis=1)
        line = jnp.broadcast_to(line.astype(jnp.float32), (8, 3 * LANES))
        return pltpu.roll(line, lax.rem(3 * LANES - offset, 3 * LANES), 1)[0:1]

    even = g - core
    own_ids = lane_ids(g)[:, :rows]
    mate_ids = lane_ids(even + 1 - core)[:, :rows]
    x_ids = lane_ids(block(1))[:, :rows]
    for q, b in enumerate((g, block(-2), block(-4))):
        COL[q] = jnp.transpose(jnp.broadcast_to(lane_ids(b)[:, : 2 * LANES], (LANES, 2 * LANES)))

    def nt(a, b):
        return lax.dot_general(a, b, (((1,), (1,)), ((), ())), preferred_element_type=jnp.float32)

    def tn(a, b):
        return lax.dot_general(a, b, (((0,), (0,)), ((), ())), preferred_element_type=jnp.float32)

    def nn(a, b):
        return jnp.dot(a, b, preferred_element_type=jnp.float32)

    def signal(q, r, student_img, teacher_img, img_ids):
        span = pl.ds(0, rows) if r is None else piece(r)
        student = (0.5 * gain) * nt(TS[q, span], student_img[...]) + 0.5 * logit_shift
        teacher = (0.5 * gain) * nt(TT[q, span], teacher_img[...]) + 0.5 * logit_shift
        same = jnp.where(COL[q, span, 0:1] == img_ids, 0.5, 0.0)
        target = same + (0.25 + 0.25 * jnp.tanh(teacher))
        return ((0.5 + 0.5 * jnp.tanh(student)) - target).astype(jnp.bfloat16)

    own = signal(0, None, IS.at[0], IT.at[0], own_ids)
    SIG[0, 0] = own
    H_OWN[...] = nn(own, IS[0])
    for copy in to_mate:
        copy.wait_recv()

    @pl.when(c0)
    def _():
        other = signal(0, None, IS.at[1], IT.at[1], mate_ids)
        SIG[0, 1] = other
        H_OWN[...] += nn(other, IS[1])

    def second(r):
        for i in range(2):
            p2[r, i].wait_recv()

            @pl.when(forwards)
            def _():
                fwd[r, i].start()

        other = signal(2, r, IS.at[1], IT.at[1], mate_ids)
        SIG[2, 1, piece(r)] = other
        H2S[piece(r)] = nn(other, IS[1]).astype(jnp.bfloat16)
        h2[r].start()

    def first(r):
        p1[r, 0].wait_recv()
        if r == 0:
            @pl.when(sends_x)
            def _():
                for copy in to_x:
                    copy.start()

        p1[r, 1].wait_recv()
        near = signal(1, r, IS.at[0], IT.at[0], own_ids)
        SIG[1, 0, piece(r)] = near
        other = signal(1, r, IS.at[1], IT.at[1], mate_ids)
        SIG[1, 1, piece(r)] = other
        H_ACC[...] = nn(near, IS[0]) + nn(other, IS[1])

        @pl.when(gets_x)
        def _():
            if r == 0:
                for copy in to_x:
                    copy.wait_recv()
            far = signal(1, r, XS, XT, x_ids)
            SIGX[piece(r)] = far
            H_ACC[...] += nn(far, XS[...])

        H1S[piece(r)] = H_ACC[...].astype(jnp.bfloat16)
        h1[r].start()

    @pl.when(has_p2)
    def _():
        second(0)

    @pl.when(has_p2 & right_x)
    def _():
        second(1)

    first(0)

    @pl.when(has_p2 & no(right_x))
    def _():
        second(1)

    first(1)

    @pl.when(gets_x)
    def _():
        GXS[...] = tn(SIGX[...], TS[1]).astype(jnp.bfloat16)
        gx_copy.start()

    G_OWN[...] = tn(SIG[1, 1], TS[1])

    @pl.when(c0)
    def _():
        G_OWN[...] += tn(SIG[0, 1], TS[0])

    @pl.when(has_p2)
    def _():
        G_OWN[...] += tn(SIG[2, 1], TS[2])

    GS[...] = G_OWN[...].astype(jnp.bfloat16)
    g_copy.start()
    G_OWN[...] = tn(SIG[0, 0], TS[0]) + tn(SIG[1, 0], TS[1])

    @pl.when(sends_x)
    def _():
        gx_copy.wait_recv()
        G_OWN[...] += GXR[...].astype(jnp.float32)

    g_copy.wait_recv()
    G_OUT[...] = (gain * (G_OWN[...] + GR[...].astype(jnp.float32))).astype(jnp.bfloat16)
    g_out.start()

    for r in range(PARTS):
        @pl.when(sends_p2)
        def _():
            h2[r].wait_recv()
            H_OWN[piece(r)] += H2R[piece(r)].astype(jnp.float32)

        h1[r].wait_recv()
        H_OUT[piece(r)] = (gain * (H_OWN[piece(r)] + H1R[piece(r)].astype(jnp.float32))).astype(jnp.bfloat16)
        h_out[r].start()

    for copy in to_mate + h1 + [g_copy]:
        copy.wait_send()

    @pl.when(sends_p1)
    def _():
        for key in p1:
            p1[key].wait_send()

    @pl.when(sends_p2)
    def _():
        for key in p2:
            p2[key].wait_send()

    @pl.when(forwards)
    def _():
        for key in fwd:
            fwd[key].wait_send()

    @pl.when(has_p2)
    def _():
        for copy in h2:
            copy.wait_send()

    @pl.when(sends_x)
    def _():
        for copy in to_x:
            copy.wait_send()

    @pl.when(gets_x)
    def _():
        gx_copy.wait_send()

    for copy in h_out + [g_out]:
        copy.wait()


def local(n_blk, n_inner, image_student, text_student, image_teacher, text_teacher, pair_ids):
    rows, width = image_student.shape
    bf, f32 = jnp.bfloat16, jnp.float32
    VM, DMA = pltpu.VMEM, pltpu.SemaphoreType.DMA
    ids = pair_ids.reshape(-1, LANES)
    part = rows // PARTS
    one = (rows, width)
    return pl.pallas_call(
        functools.partial(kernel, n_blk, n_inner),
        out_shape=(jax.ShapeDtypeStruct(one, bf), jax.ShapeDtypeStruct(one, bf)),
        in_specs=[pl.BlockSpec(memory_space=pl.ANY)] * 5,
        out_specs=(pl.BlockSpec(memory_space=pl.ANY),) * 2,
        scratch_shapes=[
            VM((2, *one), bf), VM((2, *one), bf),
            VM((3, *one), bf), VM((3, *one), bf),
            VM(one, bf), VM(one, bf),
            VM((3, 2, rows, rows), bf), VM((rows, rows), bf),
            VM(ids.shape, jnp.int32), VM((3, 2 * LANES, LANES), f32),
            VM(one, f32), VM((part, width), f32),
            VM(one, bf), VM(one, bf), VM(one, bf), VM(one, bf),
            VM(one, f32), VM(one, bf), VM(one, bf), VM(one, bf), VM(one, bf),
            VM(one, bf), VM(one, bf),
            DMA((5,)), DMA((2, 2)), DMA((2, 2)),
            DMA((2 * PARTS,)), DMA((2 * PARTS,)), DMA((2 * PARTS,)), DMA((2 * PARTS,)), DMA((2 * PARTS,)),
            DMA((2, PARTS)), DMA((2, PARTS)), DMA((2,)), DMA((2,)), DMA((PARTS + 1,)),
        ],
        compiler_params=pltpu.CompilerParams(
            collective_id=0, has_side_effects=True, vmem_limit_bytes=60 << 20
        ),
        name="window_grads",
    )(image_student, text_student, image_teacher, text_teacher, ids)


def solution(mesh):
    both = P(("blk", "inner"), None)
    return jax.shard_map(
        functools.partial(local, mesh.shape["blk"], mesh.shape["inner"]),
        mesh=mesh,
        in_specs=(both, both, both, both, P()),
        out_specs=(both, both),
        check_vma=False,
    )
```

```python
import functools

import jax
import jax.numpy as jnp
from jax import lax
from jax.experimental import pallas as pl
from jax.experimental.pallas import tpu as pltpu
from jax.sharding import PartitionSpec as P

MESH = pl.DeviceIdType.MESH
LANES = 128
PARTS = 2

logit_gain = 32.0
logit_shift = -2.0


def kernel(
    n_blk, n_inner, img_s, txt_s, img_t, txt_t, ids, image_grad, text_grad,
    IS, IT, TS, TT, XS, XT, SIG, SIGX, IDS, COL, H_OWN, H_ACC, H1S, H2S, H1R, H2R,
    G_OWN, GS, GR, GXS, GXR, G_OUT, H_OUT, RELAY,
    load_sem, img_sem, x_sem, p1_send, p1_recv, p2_send, p2_recv, fwd_send,
    h1_sem, h2_sem, g_sem, gx_sem, out_sem, relay_sem,
):
    rows, width = img_s.shape
    part = rows // PARTS
    gain = logit_gain / width
    n_dev = n_blk * n_inner
    blk, inner = lax.axis_index("blk"), lax.axis_index("inner")
    g = blk * n_inner + inner
    core = lax.rem(inner, 2)
    right_x = lax.rem(inner // 2, 2) == 1
    y = inner // 4
    top, bottom = y == n_inner // 4 - 1, y == 0
    c0, c1 = core == 0, core == 1
    no = jnp.logical_not

    has_p2 = c1 & no(bottom)
    forwards = has_p2 & right_x
    sends_p2 = c1 & no(top)
    first_one = g == 0
    wraps, wraps2 = g == n_dev - 2, g == n_dev - 3
    relays, relays2 = g == 3 * n_inner + 2, g == 4 * n_inner - 4
    sends_p1 = no(sends_p2 & right_x) & no(wraps)
    gets_h2 = sends_p2 | wraps2
    gets_x = c1 & ((right_x & top) | (no(right_x) & bottom)) & (g != n_dev - 1)
    sends_x = c0 & bottom & (g != 0)

    def block(shift):
        return lax.rem(g + shift + n_dev, n_dev)

    def at(shift):
        b = block(shift)
        return (b // n_inner, lax.rem(b, n_inner))

    def fixed(b):
        return (b // n_inner + 0 * blk, b % n_inner + 0 * inner)

    zero, relay, relay2 = fixed(0), fixed(3 * n_inner + 2), fixed(4 * n_inner - 4)
    mate = (blk, inner + 1 - 2 * core)
    after, before, after2, before2 = at(2), at(-2), at(4), at(jnp.where(first_one, -3, -4))
    step_up, step_down = at(1), at(-1)

    def piece(r):
        return pl.ds(r * part, part)

    def remote(src, dst, send, recv, to):
        return pltpu.make_async_remote_copy(
            src_ref=src, dst_ref=dst, send_sem=send, recv_sem=recv, device_id=to, device_id_type=MESH
        )

    loads = [
        pltpu.make_async_copy(src, dst, load_sem.at[i])
        for i, (src, dst) in enumerate(
            ((txt_s, TS.at[0]), (img_s, IS.at[0]), (txt_t, TT.at[0]), (img_t, IT.at[0]), (ids, IDS))
        )
    ]
    to_mate = [
        remote(src, dst, img_sem.at[0, i], img_sem.at[1, i], mate)
        for i, (src, dst) in enumerate(((img_s, IS.at[1]), (img_t, IT.at[1])))
    ]
    to_x = [
        remote(src, dst, x_sem.at[0, i], x_sem.at[1, i], step_down)
        for i, (src, dst) in enumerate(((img_s, XS), (img_t, XT)))
    ]
    p1, p2, fwd, to_relay, from_relay, to_relay2, from_relay2 = {}, {}, {}, {}, {}, {}, {}
    for r in range(PARTS):
        for i, (src, held) in enumerate(((txt_s, TS), (txt_t, TT))):
            k = 2 * r + i
            p1[r, i] = remote(src.at[piece(r)], held.at[1, piece(r)], p1_send.at[k], p1_recv.at[k], after)
            p2[r, i] = remote(src.at[piece(r)], held.at[2, piece(r)], p2_send.at[k], p2_recv.at[k], after2)
            to_relay[r, i] = remote(
                src.at[piece(r)], RELAY.at[i, piece(r)], relay_sem.at[0, k], relay_sem.at[1, k], relay
            )
            from_relay[r, i] = remote(
                RELAY.at[i, piece(r)], held.at[1, piece(r)], relay_sem.at[2, k], p1_recv.at[k], zero
            )
            to_relay2[r, i] = remote(
                src.at[piece(r)], RELAY.at[i, piece(r)], relay_sem.at[0, k], relay_sem.at[1, k], relay2
            )
            from_relay2[r, i] = remote(
                RELAY.at[i, piece(r)], held.at[2, piece(r)], relay_sem.at[2, k], p2_recv.at[k], zero
            )
            fwd[r, i] = remote(
                held.at[2, piece(r)], held.at[1, piece(r)], fwd_send.at[k], p1_recv.at[k], before
            )
    h1 = [remote(H1S.at[piece(r)], H1R.at[piece(r)], h1_sem.at[0, r], h1_sem.at[1, r], before) for r in range(PARTS)]
    h2 = [remote(H2S.at[piece(r)], H2R.at[piece(r)], h2_sem.at[0, r], h2_sem.at[1, r], before2) for r in range(PARTS)]
    g_copy = remote(GS, GR, g_sem.at[0], g_sem.at[1], mate)
    gx_copy = remote(GXS, GXR, gx_sem.at[0], gx_sem.at[1], step_up)
    g_out = pltpu.make_async_copy(G_OUT, image_grad, out_sem.at[PARTS])
    h_out = [
        pltpu.make_async_copy(H_OUT.at[piece(r)], text_grad.at[piece(r)], out_sem.at[r]) for r in range(PARTS)
    ]

    barrier = pltpu.get_barrier_semaphore()

    def greet(to):
        pl.semaphore_signal(barrier, inc=1, device_id=to, device_id_type=MESH)

    greet(mate)
    greet(before)

    @pl.when(has_p2)
    def _():
        greet(before2)

    @pl.when(has_p2 & no(right_x))
    def _():
        greet(after)

    @pl.when(gets_x)
    def _():
        greet(step_up)

    @pl.when(relays)
    def _():
        greet(fixed(n_dev - 2))

    @pl.when(relays2)
    def _():
        greet(fixed(n_dev - 3))

    @pl.when(first_one)
    def _():
        greet(relay2)

    for copy in loads:
        copy.start()
    peers = 2 + jnp.where(sends_p2, 1, 0) + jnp.where(forwards, 1, 0) + jnp.where(sends_x | wraps | wraps2 | relays2, 1, 0)
    pl.semaphore_wait(barrier, peers)

    @pl.when(sends_x)
    def _():
        for copy in to_x:
            copy.start()

    @pl.when(wraps)
    def _():
        for key in to_relay:
            to_relay[key].start()

    @pl.when(wraps2)
    def _():
        for key in to_relay2:
            to_relay2[key].start()

    @pl.when(sends_p1)
    def _():
        for key in p1:
            p1[key].start()

    @pl.when(sends_p2)
    def _():
        for key in p2:
            p2[key].start()

    for copy in to_mate:
        copy.start()

    for copy in loads:
        copy.wait()

    def lane_ids(b):
        start = b * rows
        first = jnp.minimum(start // LANES, IDS.shape[0] - 3)
        offset = start - first * LANES
        line = jnp.concatenate([IDS[pl.ds(first + i, 1), :] for i in range(3)], axis=1)
        line = jnp.broadcast_to(line.astype(jnp.float32), (8, 3 * LANES))
        return pltpu.roll(line, lax.rem(3 * LANES - offset, 3 * LANES), 1)[0:1]

    even = g - core
    own_ids = lane_ids(g)[:, :rows]
    mate_ids = lane_ids(even + 1 - core)[:, :rows]
    x_ids = lane_ids(block(1))[:, :rows]
    for q, b in enumerate((g, block(-2), block(jnp.where(first_one, -3, -4)))):
        COL[q] = jnp.transpose(jnp.broadcast_to(lane_ids(b)[:, : 2 * LANES], (LANES, 2 * LANES)))

    def nt(a, b):
        return lax.dot_general(a, b, (((1,), (1,)), ((), ())), preferred_element_type=jnp.float32)

    def tn(a, b):
        return lax.dot_general(a, b, (((0,), (0,)), ((), ())), preferred_element_type=jnp.float32)

    def nn(a, b):
        return jnp.dot(a, b, preferred_element_type=jnp.float32)

    def signal(q, r, student_img, teacher_img, img_ids):
        span = pl.ds(0, rows) if r is None else piece(r)
        student = (0.5 * gain) * nt(TS[q, span], student_img[...]) + 0.5 * logit_shift
        teacher = (0.5 * gain) * nt(TT[q, span], teacher_img[...]) + 0.5 * logit_shift
        same = jnp.where(COL[q, span, 0:1] == img_ids, 0.5, 0.0)
        target = same + (0.25 + 0.25 * jnp.tanh(teacher))
        return ((0.5 + 0.5 * jnp.tanh(student)) - target).astype(jnp.bfloat16)

    own = signal(0, None, IS.at[0], IT.at[0], own_ids)
    SIG[0, 0] = own
    H_OWN[...] = nn(own, IS[0])
    for copy in to_mate:
        copy.wait_recv()

    @pl.when(c0)
    def _():
        other = signal(0, None, IS.at[1], IT.at[1], mate_ids)
        SIG[0, 1] = other
        H_OWN[...] += nn(other, IS[1])

    def second(r, m, img_ids):
        for i in range(2):
            p2[r, i].wait_recv()

            @pl.when(forwards)
            def _():
                fwd[r, i].start()

        other = signal(2, r, IS.at[m], IT.at[m], img_ids)
        SIG[2, m, piece(r)] = other
        H2S[piece(r)] = nn(other, IS[m]).astype(jnp.bfloat16)
        h2[r].start()

    def first(r):
        for i in range(2):
            p1[r, i].wait_recv()
        near = signal(1, r, IS.at[0], IT.at[0], own_ids)
        SIG[1, 0, piece(r)] = near
        other = signal(1, r, IS.at[1], IT.at[1], mate_ids)
        SIG[1, 1, piece(r)] = other
        H_ACC[...] = nn(near, IS[0]) + nn(other, IS[1])

        @pl.when(gets_x)
        def _():
            if r == 0:
                for copy in to_x:
                    copy.wait_recv()
            far = signal(1, r, XS, XT, x_ids)
            SIGX[piece(r)] = far
            H_ACC[...] += nn(far, XS[...])

        H1S[piece(r)] = H_ACC[...].astype(jnp.bfloat16)
        h1[r].start()

    @pl.when(has_p2)
    def _():
        second(0, 1, mate_ids)

    @pl.when(has_p2 & right_x)
    def _():
        second(1, 1, mate_ids)

    first(0)

    @pl.when(has_p2 & no(right_x))
    def _():
        second(1, 1, mate_ids)

    @pl.when(relays)
    def _():
        for i in range(2):
            to_relay[0, i].wait_recv()
            from_relay[0, i].start()

    first(1)

    @pl.when(relays)
    def _():
        for i in range(2):
            to_relay[1, i].wait_recv()
            from_relay[1, i].start()

    @pl.when(relays2)
    def _():
        for key in to_relay2:
            to_relay2[key].wait_recv()
            from_relay2[key].start()

    @pl.when(gets_x)
    def _():
        GXS[...] = tn(SIGX[...], TS[1]).astype(jnp.bfloat16)
        gx_copy.start()

    G_OWN[...] = tn(SIG[1, 1], TS[1])

    @pl.when(c0)
    def _():
        G_OWN[...] += tn(SIG[0, 1], TS[0])

    @pl.when(has_p2)
    def _():
        G_OWN[...] += tn(SIG[2, 1], TS[2])

    GS[...] = G_OWN[...].astype(jnp.bfloat16)
    g_copy.start()
    G_OWN[...] = tn(SIG[0, 0], TS[0]) + tn(SIG[1, 0], TS[1])

    @pl.when(first_one)
    def _():
        second(0, 0, own_ids)
        second(1, 0, own_ids)
        G_OWN[...] += tn(SIG[2, 0], TS[2])

    @pl.when(sends_x)
    def _():
        gx_copy.wait_recv()
        G_OWN[...] += GXR[...].astype(jnp.float32)

    g_copy.wait_recv()
    G_OUT[...] = (gain * (G_OWN[...] + GR[...].astype(jnp.float32))).astype(jnp.bfloat16)
    g_out.start()

    for r in range(PARTS):
        @pl.when(gets_h2)
        def _():
            h2[r].wait_recv()
            H_OWN[piece(r)] += H2R[piece(r)].astype(jnp.float32)

        h1[r].wait_recv()
        H_OUT[piece(r)] = (gain * (H_OWN[piece(r)] + H1R[piece(r)].astype(jnp.float32))).astype(jnp.bfloat16)
        h_out[r].start()

    for copy in to_mate + h1 + [g_copy]:
        copy.wait_send()

    @pl.when(sends_p1)
    def _():
        for key in p1:
            p1[key].wait_send()

    @pl.when(wraps)
    def _():
        for key in to_relay:
            to_relay[key].wait_send()

    @pl.when(relays)
    def _():
        for key in from_relay:
            from_relay[key].wait_send()

    @pl.when(sends_p2)
    def _():
        for key in p2:
            p2[key].wait_send()

    @pl.when(forwards)
    def _():
        for key in fwd:
            fwd[key].wait_send()

    @pl.when(relays2)
    def _():
        for key in from_relay2:
            from_relay2[key].wait_send()

    @pl.when(wraps2)
    def _():
        for key in to_relay2:
            to_relay2[key].wait_send()

    @pl.when(has_p2 | first_one)
    def _():
        for copy in h2:
            copy.wait_send()

    @pl.when(sends_x)
    def _():
        for copy in to_x:
            copy.wait_send()

    @pl.when(gets_x)
    def _():
        gx_copy.wait_send()

    for copy in h_out + [g_out]:
        copy.wait()


def local(n_blk, n_inner, image_student, text_student, image_teacher, text_teacher, pair_ids):
    rows, width = image_student.shape
    bf, f32 = jnp.bfloat16, jnp.float32
    VM, DMA = pltpu.VMEM, pltpu.SemaphoreType.DMA
    ids = pair_ids.reshape(-1, LANES)
    part = rows // PARTS
    one = (rows, width)
    return pl.pallas_call(
        functools.partial(kernel, n_blk, n_inner),
        out_shape=(jax.ShapeDtypeStruct(one, bf), jax.ShapeDtypeStruct(one, bf)),
        in_specs=[pl.BlockSpec(memory_space=pl.ANY)] * 5,
        out_specs=(pl.BlockSpec(memory_space=pl.ANY),) * 2,
        scratch_shapes=[
            VM((2, *one), bf), VM((2, *one), bf),
            VM((3, *one), bf), VM((3, *one), bf),
            VM(one, bf), VM(one, bf),
            VM((3, 2, rows, rows), bf), VM((rows, rows), bf),
            VM(ids.shape, jnp.int32), VM((3, 2 * LANES, LANES), f32),
            VM(one, f32), VM((part, width), f32),
            VM(one, bf), VM(one, bf), VM(one, bf), VM(one, bf),
            VM(one, f32), VM(one, bf), VM(one, bf), VM(one, bf), VM(one, bf),
            VM(one, bf), VM(one, bf), VM((2, *one), bf),
            DMA((5,)), DMA((2, 2)), DMA((2, 2)),
            DMA((2 * PARTS,)), DMA((2 * PARTS,)), DMA((2 * PARTS,)), DMA((2 * PARTS,)), DMA((2 * PARTS,)),
            DMA((2, PARTS)), DMA((2, PARTS)), DMA((2,)), DMA((2,)), DMA((PARTS + 1,)), DMA((3, 2 * PARTS)),
        ],
        compiler_params=pltpu.CompilerParams(
            collective_id=0, has_side_effects=True, vmem_limit_bytes=60 << 20
        ),
        name="window_grads",
    )(image_student, text_student, image_teacher, text_teacher, ids)


def solution(mesh):
    both = P(("blk", "inner"), None)
    return jax.shard_map(
        functools.partial(local, mesh.shape["blk"], mesh.shape["inner"]),
        mesh=mesh,
        in_specs=(both, both, both, both, P()),
        out_specs=(both, both),
        check_vma=False,
    )
```

```python
import functools

import jax
import jax.numpy as jnp
from jax import lax
from jax.experimental import pallas as pl
from jax.experimental.pallas import tpu as pltpu
from jax.sharding import PartitionSpec as P

MESH = pl.DeviceIdType.MESH
LANES = 128
PARTS = 2

logit_gain = 32.0
logit_shift = -2.0


def kernel(
    n_blk, n_inner, img_s, txt_s, img_t, txt_t, ids, image_grad, text_grad,
    IS, IT, TS, TT, XS, XT, SIG, SIGX, IDS, COL, H_OWN, H_ACC, H1S, H2S, H1R, H2R,
    G_OWN, GS, GR, GXS, GXR, G_OUT, H_OUT, RELAY,
    load_sem, img_sem, x_sem, p1_send, p1_recv, p2_send, p2_recv, fwd_send,
    h1_sem, h2_sem, g_sem, gx_sem, out_sem, relay_sem, back_sem, go_sem,
):
    rows, width = img_s.shape
    part = rows // PARTS
    gain = logit_gain / width
    n_dev = n_blk * n_inner
    blk, inner = lax.axis_index("blk"), lax.axis_index("inner")
    g = blk * n_inner + inner
    core = lax.rem(inner, 2)
    right_x = lax.rem(inner // 2, 2) == 1
    y = inner // 4
    top, bottom = y == n_inner // 4 - 1, y == 0
    c0, c1 = core == 0, core == 1
    no = jnp.logical_not

    has_p2 = c1 & no(bottom)
    forwards = has_p2 & right_x
    sends_p2 = c1 & no(top)
    first_two, second_even = (g == 0) | (g == 2), g == 2
    passes = (g == 1) | (g == n_dev - 1)
    wraps, relays = g == n_dev - 2, g == 3 * n_inner + 2
    sends_p1 = no(sends_p2 & right_x) & no(wraps)
    gets_h2 = sends_p2 | (g == n_dev - 3) | (g == n_dev - 1)
    gets_x = c1 & ((right_x & top) | (no(right_x) & bottom)) & no(passes)
    sends_x = c0 & bottom & no(first_two)

    def block(shift):
        return lax.rem(g + shift + n_dev, n_dev)

    def at(shift):
        b = block(shift)
        return (b // n_inner, lax.rem(b, n_inner))

    def fixed(b):
        return (b // n_inner + 0 * blk, b % n_inner + 0 * inner)

    zero, relay = fixed(0), fixed(3 * n_inner + 2)
    mate = (blk, inner + 1 - 2 * core)
    after, before, after2, before2 = at(2), at(-2), at(4), at(jnp.where(first_two, -3, -4))
    step_up, step_down = at(1), at(-1)

    def piece(r):
        return pl.ds(r * part, part)

    def remote(src, dst, send, recv, to):
        return pltpu.make_async_remote_copy(
            src_ref=src, dst_ref=dst, send_sem=send, recv_sem=recv, device_id=to, device_id_type=MESH
        )

    loads = [
        pltpu.make_async_copy(src, dst, load_sem.at[i])
        for i, (src, dst) in enumerate(
            ((txt_s, TS.at[0]), (img_s, IS.at[0]), (txt_t, TT.at[0]), (img_t, IT.at[0]), (ids, IDS))
        )
    ]
    to_mate = [
        remote(src, dst, img_sem.at[0, i], img_sem.at[1, i], mate)
        for i, (src, dst) in enumerate(((img_s, IS.at[1]), (img_t, IT.at[1])))
    ]
    to_x = [
        remote(src, dst, x_sem.at[0, i], x_sem.at[1, i], step_down)
        for i, (src, dst) in enumerate(((img_s, XS), (img_t, XT)))
    ]
    p1, p2, fwd, to_relay, from_relay, ahead = {}, {}, {}, {}, {}, {}
    for r in range(PARTS):
        for i, (src, held) in enumerate(((txt_s, TS), (txt_t, TT))):
            k = 2 * r + i
            p1[r, i] = remote(src.at[piece(r)], held.at[1, piece(r)], p1_send.at[k], p1_recv.at[k], after)
            p2[r, i] = remote(src.at[piece(r)], held.at[2, piece(r)], p2_send.at[k], p2_recv.at[k], after2)
            to_relay[r, i] = remote(
                src.at[piece(r)], RELAY.at[i, piece(r)], relay_sem.at[0, k], relay_sem.at[1, k], relay
            )
            from_relay[r, i] = remote(
                RELAY.at[i, piece(r)], held.at[1, piece(r)], relay_sem.at[2, k], p1_recv.at[k], zero
            )
            ahead[r, i] = remote(
                held.at[1, piece(r)], held.at[2, piece(r)], relay_sem.at[2, k], p2_recv.at[k], step_up
            )
            fwd[r, i] = remote(
                held.at[2, piece(r)], held.at[1, piece(r)], fwd_send.at[k], p1_recv.at[k], before
            )
    h1 = [remote(H1S.at[piece(r)], H1R.at[piece(r)], h1_sem.at[0, r], h1_sem.at[1, r], before) for r in range(PARTS)]
    h2 = [remote(H2S.at[piece(r)], H2R.at[piece(r)], h2_sem.at[0, r], h2_sem.at[1, r], before2) for r in range(PARTS)]
    back = [
        remote(H2S.at[piece(r)], GXR.at[piece(r)], back_sem.at[0, r], back_sem.at[1, r], before) for r in range(PARTS)
    ]
    on = [remote(GXR.at[piece(r)], H2R.at[piece(r)], back_sem.at[2, r], h2_sem.at[1, r], step_down) for r in range(PARTS)]
    g_copy = remote(GS, GR, g_sem.at[0], g_sem.at[1], mate)
    gx_copy = remote(GXS, GXR, gx_sem.at[0], gx_sem.at[1], step_up)
    g_out = pltpu.make_async_copy(G_OUT, image_grad, out_sem.at[PARTS])
    h_out = [
        pltpu.make_async_copy(H_OUT.at[piece(r)], text_grad.at[piece(r)], out_sem.at[r]) for r in range(PARTS)
    ]

    barrier = pltpu.get_barrier_semaphore()

    def greet(to):
        pl.semaphore_signal(barrier, inc=1, device_id=to, device_id_type=MESH)

    greet(before)

    @pl.when(c1)
    def _():
        greet(mate)

    @pl.when(has_p2)
    def _():
        greet(before2)

    @pl.when(has_p2 & no(right_x))
    def _():
        greet(after)

    @pl.when(gets_x)
    def _():
        greet(step_up)

    @pl.when(relays)
    def _():
        greet(fixed(n_dev - 2))

    @pl.when(first_two)
    def _():
        greet(step_down)

    for copy in loads:
        copy.start()
    peers = 2 - core + jnp.where(sends_p2, 1, 0) + jnp.where(forwards, 1, 0) + jnp.where(sends_x | wraps | passes, 1, 0)
    pl.semaphore_wait(barrier, peers)

    @pl.when(sends_x)
    def _():
        for copy in to_x:
            copy.start()

    @pl.when(wraps)
    def _():
        for key in to_relay:
            to_relay[key].start()

    @pl.when(sends_p1 & no(second_even))
    def _():
        for key in p1:
            p1[key].start()

    @pl.when(g == 0)
    def _():
        pl.semaphore_signal(go_sem, inc=1, device_id=after, device_id_type=MESH)

    @pl.when(sends_p2)
    def _():
        for key in p2:
            p2[key].start()

    @pl.when(c0)
    def _():
        for copy in to_mate:
            copy.start()

    for copy in loads:
        copy.wait()

    def lane_ids(b):
        start = b * rows
        first = jnp.minimum(start // LANES, IDS.shape[0] - 3)
        offset = start - first * LANES
        line = jnp.concatenate([IDS[pl.ds(first + i, 1), :] for i in range(3)], axis=1)
        line = jnp.broadcast_to(line.astype(jnp.float32), (8, 3 * LANES))
        return pltpu.roll(line, lax.rem(3 * LANES - offset, 3 * LANES), 1)[0:1]

    even = g - core
    own_ids = lane_ids(g)[:, :rows]
    mate_ids = lane_ids(even + 1 - core)[:, :rows]
    x_ids = lane_ids(block(1))[:, :rows]
    for q, b in enumerate((g, block(-2), block(jnp.where(first_two, -3, -4)))):
        COL[q] = jnp.transpose(jnp.broadcast_to(lane_ids(b)[:, : 2 * LANES], (LANES, 2 * LANES)))

    def nt(a, b):
        return lax.dot_general(a, b, (((1,), (1,)), ((), ())), preferred_element_type=jnp.float32)

    def tn(a, b):
        return lax.dot_general(a, b, (((0,), (0,)), ((), ())), preferred_element_type=jnp.float32)

    def nn(a, b):
        return jnp.dot(a, b, preferred_element_type=jnp.float32)

    def signal(q, r, student_img, teacher_img, img_ids):
        span = pl.ds(0, rows) if r is None else piece(r)
        student = (0.5 * gain) * nt(TS[q, span], student_img[...]) + 0.5 * logit_shift
        teacher = (0.5 * gain) * nt(TT[q, span], teacher_img[...]) + 0.5 * logit_shift
        same = jnp.where(COL[q, span, 0:1] == img_ids, 0.5, 0.0)
        target = same + (0.25 + 0.25 * jnp.tanh(teacher))
        return ((0.5 + 0.5 * jnp.tanh(student)) - target).astype(jnp.bfloat16)

    own = signal(0, None, IS.at[0], IT.at[0], own_ids)
    SIG[0, 0] = own
    H_OWN[...] = nn(own, IS[0])
    for copy in to_mate:
        copy.wait_recv()

    @pl.when(c1)
    def _():
        for copy in to_mate:
            copy.start()

    @pl.when(c0)
    def _():
        other = signal(0, None, IS.at[1], IT.at[1], mate_ids)
        SIG[0, 1] = other
        H_OWN[...] += nn(other, IS[1])

    @pl.when(second_even)
    def _():
        pl.semaphore_wait(go_sem, 1)
        for key in p1:
            p1[key].start()

    def second(r, m, img_ids):
        for i in range(2):
            p2[r, i].wait_recv()

            @pl.when(forwards)
            def _():
                fwd[r, i].start()

        other = signal(2, r, IS.at[m], IT.at[m], img_ids)
        SIG[2, m, piece(r)] = other
        H2S[piece(r)] = nn(other, IS[m]).astype(jnp.bfloat16)

        @pl.when(second_even)
        def _():
            back[r].start()

        @pl.when(no(second_even))
        def _():
            h2[r].start()

    def first(r):
        for i in range(2):
            p1[r, i].wait_recv()

            @pl.when(passes)
            def _():
                ahead[r, i].start()

        near = signal(1, r, IS.at[0], IT.at[0], own_ids)
        SIG[1, 0, piece(r)] = near
        other = signal(1, r, IS.at[1], IT.at[1], mate_ids)
        SIG[1, 1, piece(r)] = other
        H_ACC[...] = nn(near, IS[0]) + nn(other, IS[1])

        @pl.when(gets_x)
        def _():
            if r == 0:
                for copy in to_x:
                    copy.wait_recv()
            far = signal(1, r, XS, XT, x_ids)
            SIGX[piece(r)] = far
            H_ACC[...] += nn(far, XS[...])

        H1S[piece(r)] = H_ACC[...].astype(jnp.bfloat16)
        h1[r].start()

    @pl.when(has_p2)
    def _():
        second(0, 1, mate_ids)

    @pl.when(has_p2 & right_x)
    def _():
        second(1, 1, mate_ids)

    first(0)

    @pl.when(has_p2 & no(right_x))
    def _():
        second(1, 1, mate_ids)

    @pl.when(relays)
    def _():
        for i in range(2):
            to_relay[0, i].wait_recv()
            from_relay[0, i].start()

    first(1)

    @pl.when(relays)
    def _():
        for i in range(2):
            to_relay[1, i].wait_recv()
            from_relay[1, i].start()

    @pl.when(gets_x)
    def _():
        GXS[...] = tn(SIGX[...], TS[1]).astype(jnp.bfloat16)
        gx_copy.start()

    G_OWN[...] = tn(SIG[1, 1], TS[1])

    @pl.when(c0)
    def _():
        G_OWN[...] += tn(SIG[0, 1], TS[0])

    @pl.when(has_p2)
    def _():
        G_OWN[...] += tn(SIG[2, 1], TS[2])

    GS[...] = G_OWN[...].astype(jnp.bfloat16)
    g_copy.start()
    G_OWN[...] = tn(SIG[0, 0], TS[0]) + tn(SIG[1, 0], TS[1])

    @pl.when(g == 0)
    def _():
        for r in range(PARTS):
            back[r].wait_recv()
            on[r].start()

    @pl.when(first_two)
    def _():
        second(0, 0, own_ids)
        second(1, 0, own_ids)
        G_OWN[...] += tn(SIG[2, 0], TS[2])

    @pl.when(sends_x)
    def _():
        gx_copy.wait_recv()
        G_OWN[...] += GXR[...].astype(jnp.float32)

    g_copy.wait_recv()
    G_OUT[...] = (gain * (G_OWN[...] + GR[...].astype(jnp.float32))).astype(jnp.bfloat16)
    g_out.start()

    for r in range(PARTS):
        @pl.when(gets_h2)
        def _():
            h2[r].wait_recv()
            H_OWN[piece(r)] += H2R[piece(r)].astype(jnp.float32)

        h1[r].wait_recv()
        H_OUT[piece(r)] = (gain * (H_OWN[piece(r)] + H1R[piece(r)].astype(jnp.float32))).astype(jnp.bfloat16)
        h_out[r].start()

    for copy in to_mate + h1 + [g_copy]:
        copy.wait_send()

    @pl.when(sends_p1)
    def _():
        for key in p1:
            p1[key].wait_send()

    @pl.when(wraps)
    def _():
        for key in to_relay:
            to_relay[key].wait_send()

    @pl.when(relays)
    def _():
        for key in from_relay:
            from_relay[key].wait_send()

    @pl.when(sends_p2)
    def _():
        for key in p2:
            p2[key].wait_send()

    @pl.when(forwards)
    def _():
        for key in fwd:
            fwd[key].wait_send()

    @pl.when(passes)
    def _():
        for key in ahead:
            ahead[key].wait_send()

    @pl.when(has_p2 | (g == 0))
    def _():
        for copy in h2:
            copy.wait_send()

    @pl.when(second_even)
    def _():
        for copy in back:
            copy.wait_send()

    @pl.when(g == 0)
    def _():
        for copy in on:
            copy.wait_send()

    @pl.when(sends_x)
    def _():
        for copy in to_x:
            copy.wait_send()

    @pl.when(gets_x)
    def _():
        gx_copy.wait_send()

    for copy in h_out + [g_out]:
        copy.wait()


def local(n_blk, n_inner, image_student, text_student, image_teacher, text_teacher, pair_ids):
    rows, width = image_student.shape
    bf, f32 = jnp.bfloat16, jnp.float32
    VM, DMA = pltpu.VMEM, pltpu.SemaphoreType.DMA
    ids = pair_ids.reshape(-1, LANES)
    part = rows // PARTS
    one = (rows, width)
    return pl.pallas_call(
        functools.partial(kernel, n_blk, n_inner),
        out_shape=(jax.ShapeDtypeStruct(one, bf), jax.ShapeDtypeStruct(one, bf)),
        in_specs=[pl.BlockSpec(memory_space=pl.ANY)] * 5,
        out_specs=(pl.BlockSpec(memory_space=pl.ANY),) * 2,
        scratch_shapes=[
            VM((2, *one), bf), VM((2, *one), bf),
            VM((3, *one), bf), VM((3, *one), bf),
            VM(one, bf), VM(one, bf),
            VM((3, 2, rows, rows), bf), VM((rows, rows), bf),
            VM(ids.shape, jnp.int32), VM((3, 2 * LANES, LANES), f32),
            VM(one, f32), VM((part, width), f32),
            VM(one, bf), VM(one, bf), VM(one, bf), VM(one, bf),
            VM(one, f32), VM(one, bf), VM(one, bf), VM(one, bf), VM(one, bf),
            VM(one, bf), VM(one, bf), VM((2, *one), bf),
            DMA((5,)), DMA((2, 2)), DMA((2, 2)),
            DMA((2 * PARTS,)), DMA((2 * PARTS,)), DMA((2 * PARTS,)), DMA((2 * PARTS,)), DMA((2 * PARTS,)),
            DMA((2, PARTS)), DMA((2, PARTS)), DMA((2,)), DMA((2,)), DMA((PARTS + 1,)), DMA((3, 2 * PARTS)), DMA((3, PARTS)), pltpu.SemaphoreType.REGULAR,
        ],
        compiler_params=pltpu.CompilerParams(
            collective_id=0, has_side_effects=True, vmem_limit_bytes=48 << 20
        ),
        name="window_grads",
    )(*[pltpu.with_memory_space_constraint(a, pltpu.HBM) for a in (image_student, text_student, image_teacher, text_teacher, ids)])


def solution(mesh):
    both = P(("blk", "inner"), None)
    return jax.shard_map(
        functools.partial(local, mesh.shape["blk"], mesh.shape["inner"]),
        mesh=mesh,
        in_specs=(both, both, both, both, P()),
        out_specs=(both, both),
        check_vma=False,
    )
```
